32 devices in a mesh: layer: 4 (over y, core), lat: 8 (over z, x).
Axes of the slice: x: 2, y: 2, z: 4, core: 2. Of those that a mesh axis runs over, the one named last changes fastest.
Arguments:
- resid_halves: bfloat16 [4, 1024, 4096], P('layer'), may hold values from -6 to 6
- enc_weight: bfloat16 [4, 4096, 16384], P('layer', None, 'lat'), may hold values from -0.0625 to 0.0625
- enc_bias: float32 [2, 16384], P(None, 'lat'), may hold values from -3 to 3
- jump_threshold: float32 [2, 16384], P(None, 'lat'), may hold values from 0.1 to 1
- dec_weight: bfloat16 [4, 2, 16384, 8192], P('layer', None, 'lat'), may hold values from -0.03125 to 0.03125
- dec_bias: float32 [4, 8192], P('layer'), may hold values from -3 to 3
- clamp_rows: int32 [2, 1024], replicated, may hold values from 0 to 1023, each once within a row
- clamp_feats: int32 [2, 1024], replicated, may hold values from 0 to 16383
- clamp_slots: int32 [2, 1024], replicated, may hold values from 0 to 15
- clamp_values: float32 [16], replicated, may hold values from 5 to 15
Outputs:
- recon: bfloat16 [4, 1024, 8192], P('layer', 'lat')
The draws below stay inside these ranges and needn't reach their ends.
Inputs may be any that keep to these rules, and one draw needn't show every extreme that they name: Each row of clamp_rows names every token row once.
All inputs are finite; a program needn't handle non-finite values.
Results may differ from the reference program's by a relative error of at most 0.0042.
Values may be sent and summed in bfloat16 or wider, within the bound.
A program may use at most 192 MiB of HBM per device.

```python
import math
import jax
import jax.numpy as jnp

D = 8192
DH = 4096
LAT = 16384
TOK = 1024
NV = 16


def touch_ends(entries, stream_key, least, top_value):
    shape = entries.shape
    spot = [jax.random.randint(jax.random.fold_in(stream_key, axis), (), 0, shape[axis]) for axis in range(len(shape))]
    entries = entries.at[tuple(spot)].set(least)
    longest = shape.index(max(shape))
    spot[longest] = (spot[longest] + 1) % shape[longest]
    return entries.at[tuple(spot)].set(top_value)


def block_levels(stream_key, shape, pieces, low, largest):
    def one(dim, shards_of):
        draws = jax.random.uniform(jax.random.fold_in(jax.random.fold_in(stream_key, 6), dim), (shards_of,), jnp.float32, low / len(pieces), largest / len(pieces))
        return jnp.repeat(jnp.exp(draws), shape[dim] // shards_of).reshape((-1,) + (1,) * (len(shape) - dim - 1))

    level = one(*pieces[0])
    for cut in pieces[1:]:
        level = level * one(*cut)
    return level


def bell_draw(stream_key, shape, spread, reach, shards=(), dtype=jnp.bfloat16):
    array = spread * jax.random.normal(stream_key, shape, jnp.float32)
    if shards:
        array = array * block_levels(stream_key, shape, shards, -0.22, 0.18)
    return jnp.clip(array, -reach, reach).astype(dtype)


def setup_inputs(seed: int = 0) -> dict:
    key_of = jax.random.split(jax.random.key(seed), 11)
    return {
        "resid_halves": bell_draw(key_of[0], (4, TOK, DH), 1.0, 6.0, ((0, 4),)),
        "enc_weight": bell_draw(key_of[1], (4, DH, LAT), D ** -0.5, 0.0625, ((0, 4), (2, 8))),
        "enc_bias": bell_draw(key_of[2], (2, LAT), 0.5, 3.0, ((1, 8),), jnp.float32),
        "jump_threshold": jnp.clip(jnp.exp(math.log(1.0) - 2.3025851 * jax.random.uniform(key_of[3], (2, LAT), jnp.float32) ** block_levels(key_of[3], (2, LAT), ((1, 8),), -0.2, 0.2)), 0.1, 1.0),
        "dec_weight": bell_draw(key_of[4], (4, 2, LAT, D), (2 * LAT) ** -0.5, 0.03125, ((0, 4), (2, 8))),
        "dec_bias": bell_draw(key_of[5], (4, D), 0.5, 3.0, ((0, 4),), jnp.float32),
        "clamp_rows": jax.vmap(lambda own: jax.random.permutation(own, TOK))(jax.random.split(key_of[6], 2)).reshape((2, TOK)).astype(jnp.int32),
        "clamp_feats": touch_ends(jax.random.randint(key_of[7], (2, TOK), 0, LAT), jax.random.fold_in(key_of[7], 1), 0, LAT - 1).astype(jnp.int32),
        "clamp_slots": touch_ends(jax.random.randint(key_of[8], (2, TOK), 0, NV), jax.random.fold_in(key_of[8], 1), 0, NV - 1).astype(jnp.int32),
        "clamp_values": jnp.clip(jax.random.uniform(key_of[9], (NV,), jnp.float32, 5.0, 15.0), 5.0, 15.0),
    }


def reference(resid_halves, enc_weight, enc_bias, jump_threshold, dec_weight, dec_bias, clamp_rows, clamp_feats, clamp_slots, clamp_values):
    code_list = []
    for source in range(2):
        inputs = jnp.concatenate([resid_halves[2 * source], resid_halves[2 * source + 1]], axis=1)
        weights = jnp.concatenate([enc_weight[2 * source], enc_weight[2 * source + 1]], axis=0)
        pre_act = jnp.dot(inputs, weights, preferred_element_type=jnp.float32) + enc_bias[source][None, :]
        ramp = jnp.clip((pre_act - jump_threshold[source][None, :]) / 0.25 + 1.0, 0.0, 1.0)
        activity = pre_act * ramp
        chosen = clamp_values[clamp_slots[source]]
        activity = activity.at[clamp_rows[source], clamp_feats[source]].set(chosen)
        code_list.append(activity.astype(jnp.bfloat16))
    outputs = []
    for target in range(4):
        total = jnp.dot(code_list[0], dec_weight[target, 0], preferred_element_type=jnp.float32)
        total = total + jnp.dot(code_list[1], dec_weight[target, 1], preferred_element_type=jnp.float32)
        outputs.append((total + dec_bias[target][None, :]).astype(jnp.bfloat16))
    return jnp.stack(outputs, axis=0)
```

```python
import functools

import jax
import jax.numpy as jnp
from jax import lax
from jax.experimental import pallas as pl
from jax.experimental.pallas import tpu as pltpu
from jax.sharding import PartitionSpec as P

MESH = pl.DeviceIdType.MESH
BLOCK = 256
RING = 4
LAG = 3


def swapped(value, axis, distance):
    mask = 2**distance
    pairs = [(source, source ^ mask) for source in range(lax.axis_size(axis))]
    return lax.ppermute(value, axis, pairs)


def decode_kernel(
    n_lat, codes, weight, bias, out,
    wbuf, send1, recv1, kept, send2, recv2, mine,
    w_sem, s1_sem, r1_sem, s2_sem, r2_sem,
):
    outer = n_lat // 2
    rows = out.shape[0]
    steps = out.shape[1] // BLOCK
    me = lax.axis_index("lat")
    side = lax.rem(me, 2)
    place = me // 2
    partner = place * 2 + (1 - side)
    peers = [lax.rem(place + k, outer) * 2 + side for k in range(1, outer)]

    def columns(j):
        return pl.ds(pl.multiple_of(j * BLOCK, BLOCK), BLOCK)

    def load(j):
        return pltpu.make_async_copy(
            weight.at[:, :, columns(j)], wbuf.at[lax.rem(j, 2)], w_sem.at[lax.rem(j, 2)]
        )

    def swap(j):
        slot = lax.rem(j, RING)
        return pltpu.make_async_remote_copy(
            src_ref=send1.at[slot], dst_ref=recv1.at[j],
            send_sem=s1_sem.at[slot], recv_sem=r1_sem.at[j],
            device_id={"lat": partner}, device_id_type=MESH,
        )

    def spread(j, k):
        slot = lax.rem(j, RING)
        return pltpu.make_async_remote_copy(
            src_ref=send2.at[slot, k - 1], dst_ref=recv2.at[j, k - 1],
            send_sem=s2_sem.at[slot, k - 1], recv_sem=r2_sem.at[j, k - 1],
            device_id={"lat": peers[k - 1]}, device_id_type=MESH,
        )

    load(0).start()
    barrier = pltpu.get_barrier_semaphore()
    for device in [partner] + peers:
        pl.semaphore_signal(barrier, inc=1, device_id={"lat": device}, device_id_type=MESH)
    pl.semaphore_wait(barrier, outer)

    def partial(half, slot):
        return jnp.dot(
            codes[0, half], wbuf[slot, 0], preferred_element_type=jnp.float32
        ) + jnp.dot(codes[1, half], wbuf[slot, 1], preferred_element_type=jnp.float32)

    def step(t, carry):
        @pl.when(t < steps)
        def _():
            slot = lax.rem(t, 2)

            @pl.when(t + 1 < steps)
            def _():
                load(t + 1).start()

            load(t).wait()

            @pl.when(t >= RING)
            def _():
                swap(t - RING).wait_send()

            send1[lax.rem(t, RING)] = partial(1 - side, slot).astype(jnp.bfloat16)
            swap(t).start()
            kept[lax.rem(t, RING)] = partial(side, slot)

        u = t - LAG

        @pl.when((u >= 0) & (u < steps))
        def _():
            slot = lax.rem(u, RING)
            swap(u).wait_recv()

            @pl.when(u >= RING)
            def _():
                for k in range(1, outer):
                    spread(u - RING, k).wait_send()

            def total(where):
                span = pl.ds(pl.multiple_of(where * rows, rows), rows)
                return kept[slot, span, :] + recv1[u, span, :].astype(jnp.float32)

            for k in range(1, outer):
                send2[slot, k - 1] = total(lax.rem(place + k, outer)).astype(jnp.bfloat16)
                spread(u, k).start()
            mine[slot] = total(place)

        v = t - 2 * LAG

        @pl.when((v >= 0) & (v < steps))
        def _():
            result = mine[lax.rem(v, RING)] + bias[0, columns(v)][None, :]
            for k in range(1, outer):
                spread(v, k).wait_recv()
                result = result + recv2[v, k - 1].astype(jnp.float32)
            out[:, columns(v)] = result.astype(jnp.bfloat16)

        return carry

    lax.fori_loop(0, steps + 2 * LAG, step, 0)
    for j in range(steps - RING, steps):
        swap(j).wait_send()
        for k in range(1, outer):
            spread(j, k).wait_send()


def decode(codes, weight, bias, n_lat):
    _, _, half_rows, width = codes.shape
    model = weight.shape[2]
    steps = model // BLOCK
    outer = n_lat // 2
    rows = half_rows // outer
    vmem = pl.BlockSpec(memory_space=pltpu.VMEM)
    dma = pltpu.SemaphoreType.DMA
    return pl.pallas_call(
        functools.partial(decode_kernel, n_lat),
        out_shape=jax.ShapeDtypeStruct((rows, model), jnp.bfloat16),
        in_specs=[vmem, pl.BlockSpec(memory_space=pl.ANY), vmem],
        out_specs=vmem,
        scratch_shapes=[
            pltpu.VMEM((2, 2, width, BLOCK), jnp.bfloat16),
            pltpu.VMEM((RING, half_rows, BLOCK), jnp.bfloat16),
            pltpu.VMEM((steps, half_rows, BLOCK), jnp.bfloat16),
            pltpu.VMEM((RING, half_rows, BLOCK), jnp.float32),
            pltpu.VMEM((RING, outer - 1, rows, BLOCK), jnp.bfloat16),
            pltpu.VMEM((steps, outer - 1, rows, BLOCK), jnp.bfloat16),
            pltpu.VMEM((RING, rows, BLOCK), jnp.float32),
            dma((2,)),
            dma((RING,)),
            dma((steps,)),
            dma((RING, outer - 1)),
            dma((steps, outer - 1)),
        ],
        compiler_params=pltpu.CompilerParams(
            collective_id=0, has_side_effects=True, vmem_limit_bytes=54 * 2**20
        ),
        cost_estimate=pl.CostEstimate(
            flops=2 * 2 * half_rows * 2 * width * model,
            bytes_accessed=2 * 2 * width * model,
            transcendentals=0,
        ),
    )(codes, weight, bias)


def by_side(rows, n_lat):
    cut = rows.reshape((n_lat // 2, 2, rows.shape[0] // n_lat) + rows.shape[1:])
    return jnp.swapaxes(cut, 0, 1).reshape((2, rows.shape[0] // 2) + rows.shape[1:])


def shards(
    resid_halves,
    enc_weight,
    enc_bias,
    jump_threshold,
    dec_weight,
    dec_bias,
    clamp_rows,
    clamp_feats,
    clamp_slots,
    clamp_values,
):
    n_lat = lax.axis_size("lat")
    group = lax.axis_index("layer")
    source = group // 2
    core = lax.rem(group, 2)
    tokens = resid_halves.shape[1]
    width = enc_weight.shape[2]
    lat_first = lax.axis_index("lat") * width

    def pick(stacked, at):
        return lax.dynamic_index_in_dim(stacked, at, 0, keepdims=False)

    my_bias = pick(enc_bias, source)
    my_thresh = pick(jump_threshold, source)
    my_slots = pick(clamp_slots, source)
    slot_hot = my_slots[:, None] == jnp.arange(clamp_values.shape[0], dtype=jnp.int32)[None, :]
    chosen = jnp.sum(jnp.where(slot_hot, clamp_values[None, :], 0.0), axis=1)
    row_hot = pick(clamp_rows, source)[:, None] == jnp.arange(tokens, dtype=jnp.int32)[None, :]
    feat_row = jnp.sum(jnp.where(row_hot, pick(clamp_feats, source)[:, None], 0), axis=0)
    value_row = jnp.sum(jnp.where(row_hot, chosen[:, None], 0.0), axis=0)
    feat_row = by_side(feat_row, n_lat)
    value_row = by_side(value_row, n_lat)

    partial_pre = jnp.dot(
        by_side(resid_halves[0], n_lat).reshape(tokens, -1), enc_weight[0],
        preferred_element_type=jnp.float32,
    ).reshape(2, tokens // 2, width)
    partner = swapped(pick(partial_pre, 1 - core), "layer", 0)
    pre_act = pick(partial_pre, core) + partner + my_bias[None, :]
    ramp = jnp.clip((pre_act - my_thresh[None, :]) / 0.25 + 1.0, 0.0, 1.0)
    hit = (pick(feat_row, core) - lat_first)[:, None] == jnp.arange(width, dtype=jnp.int32)[None, :]
    half = jnp.where(hit, pick(value_row, core)[:, None], pre_act * ramp).astype(jnp.bfloat16)
    other = swapped(half, "layer", 1)
    held = jnp.where(source == 0, jnp.stack([half, other]), jnp.stack([other, half]))
    taken = swapped(held, "layer", 0)
    codes = jnp.where(
        core == 0, jnp.stack([held, taken], axis=1), jnp.stack([taken, held], axis=1)
    )
    return decode(codes, dec_weight[0], dec_bias, n_lat)[None]


def solution(mesh):
    return jax.shard_map(
        shards,
        mesh=mesh,
        in_specs=(
            P("layer", None, None),
            P("layer", None, "lat"),
            P(None, "lat"),
            P(None, "lat"),
            P("layer", None, "lat", None),
            P("layer", None),
            P(),
            P(),
            P(),
            P(),
        ),
        out_specs=P("layer", "lat", None),
        check_vma=False,
    )
```

```python
import functools

import jax
import jax.numpy as jnp
from jax import lax
from jax.experimental import pallas as pl
from jax.experimental.pallas import tpu as pltpu
from jax.sharding import PartitionSpec as P

MESH = pl.DeviceIdType.MESH
PASSES = 2
BLOCK = 512
RING = 4
LAG = 3


def swapped(value, axis, distance):
    mask = 2**distance
    pairs = [(source, source ^ mask) for source in range(lax.axis_size(axis))]
    return lax.ppermute(value, axis, pairs)


def decode_kernel(stages, half, weight, bias, out, *scratch):
    codes, wbuf, own_sem, w_sem, give_sem, take_sem = scratch[:6]
    kept, sent, got, s_sem, r_sem = (scratch[6 + i * stages : 6 + (i + 1) * stages] for i in range(5))
    rows = out.shape[0] // PASSES
    blocks = out.shape[1] // BLOCK
    steps = PASSES * blocks
    me = lax.axis_index("lat")
    group = lax.axis_index("layer")
    source, core = group // 2, lax.rem(group, 2)
    sibling = source * 2 + (1 - core)
    across = (1 - source) * 2 + core
    bits = [lax.rem(me // 2**i, 2) for i in range(stages)]
    mates = [me + (1 - 2 * bits[i]) * 2**i for i in range(stages)]

    def columns(t):
        return pl.ds(pl.multiple_of(lax.rem(t, blocks) * BLOCK, BLOCK), BLOCK)

    def load(t):
        return pltpu.make_async_copy(
            weight.at[:, :, columns(t)], wbuf.at[lax.rem(t, 2)], w_sem.at[lax.rem(t, 2)]
        )

    def settle(p):
        return pltpu.make_async_copy(half.at[p], codes.at[p, source, core], own_sem.at[p])

    def give(p, kind):
        of, to = ((source, sibling), (source, across), (1 - source, sibling))[kind]
        piece = codes.at[p, of, core]
        return pltpu.make_async_remote_copy(
            src_ref=piece, dst_ref=piece,
            send_sem=give_sem.at[p, kind], recv_sem=take_sem.at[p, kind],
            device_id={"layer": to}, device_id_type=MESH,
        )

    def take(p, kind):
        of, side = ((source, 1 - core), (1 - source, core), (1 - source, 1 - core))[kind]
        piece = codes.at[p, of, side]
        return pltpu.make_async_remote_copy(
            src_ref=piece, dst_ref=piece,
            send_sem=give_sem.at[p, kind], recv_sem=take_sem.at[p, kind],
            device_id={"layer": sibling}, device_id_type=MESH,
        )

    def pass_on(t, i):
        slot = lax.rem(t, RING)
        return pltpu.make_async_remote_copy(
            src_ref=sent[i].at[slot], dst_ref=got[i].at[t],
            send_sem=s_sem[i].at[slot], recv_sem=r_sem[i].at[t],
            device_id={"lat": mates[i]}, device_id_type=MESH,
        )

    for p in range(PASSES):
        settle(p).start()
    load(0).start()
    barrier = pltpu.get_barrier_semaphore()
    for device in [{"lat": mate} for mate in mates] + [{"layer": sibling}, {"layer": across}]:
        pl.semaphore_signal(barrier, inc=1, device_id=device, device_id_type=MESH)
    pl.semaphore_wait(barrier, stages + 2)

    settle(0).wait()
    give(0, 1).start()
    give(0, 0).start()
    settle(1).wait()
    take(0, 1).wait_recv()
    give(0, 2).start()
    give(1, 1).start()
    give(1, 0).start()
    take(0, 0).wait_recv()
    take(0, 2).wait_recv()

    def step(t, carry):
        @pl.when(t == blocks // 2)
        def _():
            take(1, 1).wait_recv()
            give(1, 2).start()

        @pl.when(t == blocks)
        def _():
            take(1, 0).wait_recv()
            take(1, 2).wait_recv()

        @pl.when(t < steps)
        def _():
            slot, p = lax.rem(t, 2), t // blocks

            def partial(side):
                return jnp.dot(
                    codes[p, 0, side], wbuf[slot, 0], preferred_element_type=jnp.float32
                ) + jnp.dot(codes[p, 1, side], wbuf[slot, 1], preferred_element_type=jnp.float32)

            @pl.when(t + 1 < steps)
            def _():
                load(t + 1).start()

            load(t).wait()

            @pl.when(t >= RING)
            def _():
                pass_on(t - RING, 0).wait_send()

            sent[0][lax.rem(t, RING)] = partial(1 - bits[0]).astype(jnp.bfloat16)
            pass_on(t, 0).start()
            kept[0][lax.rem(t, RING)] = partial(bits[0])

        for i in range(1, stages + 1):
            u = t - i * LAG

            @pl.when((u >= 0) & (u < steps))
            def _(i=i, u=u):
                slot = lax.rem(u, RING)
                pass_on(u, i - 1).wait_recv()

                def total(bit, size):
                    span = pl.ds(pl.multiple_of(bit * size, size), size)
                    return kept[i - 1][slot, span, :] + got[i - 1][u, span, :].astype(jnp.float32)

                if i < stages:
                    size = kept[i].shape[1]

                    @pl.when(u >= RING)
                    def _():
                        pass_on(u - RING, i).wait_send()

                    sent[i][slot] = total(1 - bits[i], size).astype(jnp.bfloat16)
                    pass_on(u, i).start()
                    kept[i][slot] = total(bits[i], size)
                else:
                    span = pl.ds(pl.multiple_of((u // blocks) * rows, rows), rows)
                    result = total(0, rows) + bias[0, columns(u)][None, :]
                    out[span, columns(u)] = result.astype(jnp.bfloat16)

        return carry

    lax.fori_loop(0, steps + stages * LAG, step, 0)
    for i in range(stages):
        for t in range(steps - RING, steps):
            pass_on(t, i).wait_send()
    for p in range(PASSES):
        for kind in range(3):
            give(p, kind).wait_send()


def decode(half, weight, bias, n_lat):
    _, part, width = half.shape
    model = weight.shape[2]
    steps = PASSES * (model // BLOCK)
    stages = n_lat.bit_length() - 1
    rows = PASSES * 2 * part // n_lat
    sizes = [part // 2**i for i in range(stages)]
    dma = pltpu.SemaphoreType.DMA
    vmem = pl.BlockSpec(memory_space=pltpu.VMEM)
    hbm = pl.BlockSpec(memory_space=pl.ANY)
    return pl.pallas_call(
        functools.partial(decode_kernel, stages),
        out_shape=jax.ShapeDtypeStruct((rows, model), jnp.bfloat16),
        in_specs=[hbm, hbm, vmem],
        out_specs=vmem,
        scratch_shapes=[
            pltpu.VMEM((PASSES, 2, 2, part, width), jnp.bfloat16),
            pltpu.VMEM((2, 2, width, BLOCK), jnp.bfloat16),
            dma((PASSES,)),
            dma((2,)),
            dma((PASSES, 3)),
            dma((PASSES, 3)),
            *(pltpu.VMEM((RING, size, BLOCK), jnp.float32) for size in sizes),
            *(pltpu.VMEM((RING, size, BLOCK), jnp.bfloat16) for size in sizes),
            *(pltpu.VMEM((steps, size, BLOCK), jnp.bfloat16) for size in sizes),
            *(dma((RING,)) for _ in sizes),
            *(dma((steps,)) for _ in sizes),
        ],
        compiler_params=pltpu.CompilerParams(
            collective_id=0, has_side_effects=True, vmem_limit_bytes=54 * 2**20
        ),
        cost_estimate=pl.CostEstimate(
            flops=2 * 2 * PASSES * part * 2 * width * model,
            bytes_accessed=PASSES * 2 * 2 * width * model,
            transcendentals=0,
        ),
    )(half, weight, bias)


def of_side(values, n_lat, side):
    stages = n_lat.bit_length() - 1
    tail = values.shape[1:]
    rows = values.shape[0] // n_lat // PASSES
    cut = values.reshape((n_lat // 2, 2, PASSES * rows) + tail)
    cut = lax.dynamic_index_in_dim(cut, side, 1, keepdims=False)
    cut = cut.reshape((2,) * (stages - 1) + (PASSES, rows) + tail)
    order = (stages - 1,) + tuple(range(stages - 2, -1, -1)) + tuple(range(stages, cut.ndim))
    return cut.transpose(order).reshape((PASSES * rows * n_lat // 2,) + tail)


def shards(
    resid_halves,
    enc_weight,
    enc_bias,
    jump_threshold,
    dec_weight,
    dec_bias,
    clamp_rows,
    clamp_feats,
    clamp_slots,
    clamp_values,
):
    n_lat = lax.axis_size("lat")
    group = lax.axis_index("layer")
    source = group // 2
    core = lax.rem(group, 2)
    tokens = resid_halves.shape[1]
    width = enc_weight.shape[2]
    lat_first = lax.axis_index("lat") * width

    def pick(stacked, at):
        return lax.dynamic_index_in_dim(stacked, at, 0, keepdims=False)

    my_bias = pick(enc_bias, source)
    my_thresh = pick(jump_threshold, source)
    my_slots = pick(clamp_slots, source)
    slot_hot = my_slots[:, None] == jnp.arange(clamp_values.shape[0], dtype=jnp.int32)[None, :]
    chosen = jnp.sum(jnp.where(slot_hot, clamp_values[None, :], 0.0), axis=1)
    row_hot = pick(clamp_rows, source)[:, None] == jnp.arange(tokens, dtype=jnp.int32)[None, :]
    feat_row = jnp.sum(jnp.where(row_hot, pick(clamp_feats, source)[:, None], 0), axis=0)
    value_row = jnp.sum(jnp.where(row_hot, chosen[:, None], 0.0), axis=0)
    feat_row = of_side(feat_row, n_lat, core)
    value_row = of_side(value_row, n_lat, core)

    partial_pre = jnp.dot(resid_halves[0], enc_weight[0], preferred_element_type=jnp.float32)
    partner = swapped(of_side(partial_pre, n_lat, 1 - core), "layer", 0)
    pre_act = of_side(partial_pre, n_lat, core) + partner + my_bias[None, :]
    ramp = jnp.clip((pre_act - my_thresh[None, :]) / 0.25 + 1.0, 0.0, 1.0)
    hit = (feat_row - lat_first)[:, None] == jnp.arange(width, dtype=jnp.int32)[None, :]
    half = jnp.where(hit, value_row[:, None], pre_act * ramp).astype(jnp.bfloat16)
    half = half.reshape(PASSES, tokens // 2 // PASSES, width)
    return decode(half, dec_weight[0], dec_bias, n_lat)[None]


def solution(mesh):
    return jax.shard_map(
        shards,
        mesh=mesh,
        in_specs=(
            P("layer", None, None),
            P("layer", None, "lat"),
            P(None, "lat"),
            P(None, "lat"),
            P("layer", None, "lat", None),
            P("layer", None),
            P(),
            P(),
            P(),
            P(),
        ),
        out_specs=P("layer", "lat", None),
        check_vma=False,
    )
```

```python
import functools

import jax
import jax.numpy as jnp
from jax import lax
from jax.experimental import pallas as pl
from jax.experimental.pallas import tpu as pltpu
from jax.sharding import PartitionSpec as P

MESH = pl.DeviceIdType.MESH
PASSES = 2
BLOCK = 512
RING = 5
LAG = 4


def swapped(value, axis, distance):
    mask = 2**distance
    pairs = [(source, source ^ mask) for source in range(lax.axis_size(axis))]
    return lax.ppermute(value, axis, pairs)


def decode_kernel(stages, half, weight, bias, out, *scratch):
    codes, wbuf, own_sem, w_sem, give_sem, take_sem = scratch[:6]
    kept, sent, got, s_sem, r_sem = (scratch[6 + i * stages : 6 + (i + 1) * stages] for i in range(5))
    rows = out.shape[0] // PASSES
    blocks = out.shape[1] // BLOCK
    steps = PASSES * blocks
    me = lax.axis_index("lat")
    group = lax.axis_index("layer")
    source, core = group // 2, lax.rem(group, 2)
    sibling = source * 2 + (1 - core)
    across = (1 - source) * 2 + core
    bits = [lax.rem(me // 2**i, 2) for i in range(stages)]
    mates = [me + (1 - 2 * bits[i]) * 2**i for i in range(stages)]

    def bit_at(t, i):
        return lax.rem(t + 2, 4) // 3 * (1 - 2 * i) + i if i < 2 else i

    def chosen(values, t, i):
        return values[0] + bit_at(t, i) * (values[1] - values[0]) if i < 2 else values[i]

    def columns(t):
        return pl.ds(pl.multiple_of(lax.rem(t, blocks) * BLOCK, BLOCK), BLOCK)

    def load(t):
        return pltpu.make_async_copy(
            weight.at[:, :, columns(t)], wbuf.at[lax.rem(t, 2)], w_sem.at[lax.rem(t, 2)]
        )

    def settle(p):
        return pltpu.make_async_copy(half.at[p], codes.at[p, source, core], own_sem.at[p])

    def give(p, kind):
        of, to = ((source, sibling), (source, across), (1 - source, sibling))[kind]
        piece = codes.at[p, of, core]
        return pltpu.make_async_remote_copy(
            src_ref=piece, dst_ref=piece,
            send_sem=give_sem.at[p, kind], recv_sem=take_sem.at[p, kind],
            device_id={"layer": to}, device_id_type=MESH,
        )

    def take(p, kind):
        of, side = ((source, 1 - core), (1 - source, core), (1 - source, 1 - core))[kind]
        piece = codes.at[p, of, side]
        return pltpu.make_async_remote_copy(
            src_ref=piece, dst_ref=piece,
            send_sem=give_sem.at[p, kind], recv_sem=take_sem.at[p, kind],
            device_id={"layer": sibling}, device_id_type=MESH,
        )

    def pass_on(t, i):
        slot = lax.rem(t, RING)
        return pltpu.make_async_remote_copy(
            src_ref=sent[i].at[slot], dst_ref=got[i].at[t],
            send_sem=s_sem[i].at[slot], recv_sem=r_sem[i].at[t],
            device_id={"lat": chosen(mates, t, i)}, device_id_type=MESH,
        )

    for p in range(PASSES):
        settle(p).start()
    load(0).start()
    barrier = pltpu.get_barrier_semaphore()
    for device in [{"lat": mate} for mate in mates] + [{"layer": sibling}, {"layer": across}]:
        pl.semaphore_signal(barrier, inc=1, device_id=device, device_id_type=MESH)
    pl.semaphore_wait(barrier, stages + 2)

    settle(0).wait()
    give(0, 1).start()
    give(0, 0).start()
    settle(1).wait()
    take(0, 1).wait_recv()
    give(0, 2).start()
    give(1, 1).start()
    give(1, 0).start()
    take(0, 0).wait_recv()
    take(0, 2).wait_recv()

    def step(t, carry):
        @pl.when(t == blocks // 2)
        def _():
            take(1, 1).wait_recv()
            give(1, 2).start()

        @pl.when(t == blocks)
        def _():
            take(1, 0).wait_recv()
            take(1, 2).wait_recv()

        @pl.when(t < steps)
        def _():
            slot, p = lax.rem(t, 2), t // blocks

            second = bit_at(t, 0)

            def picked(s, bit):
                return jnp.concatenate(
                    [codes[p, s, bit + second * (q - bit), q + second * (bit - q)] for q in range(2)], axis=0
                )

            def partial(bit):
                return jnp.dot(
                    picked(0, bit), wbuf[slot, 0], preferred_element_type=jnp.float32
                ) + jnp.dot(picked(1, bit), wbuf[slot, 1], preferred_element_type=jnp.float32)

            mine = chosen(bits, t, 0)

            @pl.when(t + 1 < steps)
            def _():
                load(t + 1).start()

            load(t).wait()

            @pl.when(t >= RING)
            def _():
                pass_on(t - RING, 0).wait_send()

            sent[0][lax.rem(t, RING)] = partial(1 - mine).astype(jnp.bfloat16)
            pass_on(t, 0).start()
            kept[0][lax.rem(t, RING)] = partial(mine)

        for i in range(1, stages + 1):
            u = t - i * LAG

            @pl.when((u >= 0) & (u < steps))
            def _(i=i, u=u):
                slot = lax.rem(u, RING)
                pass_on(u, i - 1).wait_recv()

                def total(bit, size):
                    span = pl.ds(pl.multiple_of(bit * size, size), size)
                    return kept[i - 1][slot, span, :] + got[i - 1][u, span, :].astype(jnp.float32)

                if i < stages:
                    size = kept[i].shape[1]

                    @pl.when(u >= RING)
                    def _():
                        pass_on(u - RING, i).wait_send()

                    sent[i][slot] = total(1 - chosen(bits, u, i), size).astype(jnp.bfloat16)
                    pass_on(u, i).start()
                    kept[i][slot] = total(chosen(bits, u, i), size)
                else:
                    span = pl.ds(pl.multiple_of((u // blocks) * rows, rows), rows)
                    result = total(0, rows) + bias[0, columns(u)][None, :]
                    out[span, columns(u)] = result.astype(jnp.bfloat16)

        return carry

    lax.fori_loop(0, steps + stages * LAG, step, 0)
    for i in range(stages):
        for t in range(steps - RING, steps):
            pass_on(t, i).wait_send()
    for p in range(PASSES):
        for kind in range(3):
            give(p, kind).wait_send()


def decode(half, weight, bias, n_lat):
    _, _, quarter, width = half.shape
    part = 2 * quarter
    model = weight.shape[2]
    steps = PASSES * (model // BLOCK)
    stages = n_lat.bit_length() - 1
    rows = PASSES * 2 * part // n_lat
    sizes = [part // 2**i for i in range(stages)]
    dma = pltpu.SemaphoreType.DMA
    vmem = pl.BlockSpec(memory_space=pltpu.VMEM)
    hbm = pl.BlockSpec(memory_space=pl.ANY)
    return pl.pallas_call(
        functools.partial(decode_kernel, stages),
        out_shape=jax.ShapeDtypeStruct((rows, model), jnp.bfloat16),
        in_specs=[hbm, hbm, vmem],
        out_specs=vmem,
        scratch_shapes=[
            pltpu.VMEM((PASSES, 2, 2, 2, quarter, width), jnp.bfloat16),
            pltpu.VMEM((2, 2, width, BLOCK), jnp.bfloat16),
            dma((PASSES,)),
            dma((2,)),
            dma((PASSES, 3)),
            dma((PASSES, 3)),
            *(pltpu.VMEM((RING, size, BLOCK), jnp.float32) for size in sizes),
            *(pltpu.VMEM((RING, size, BLOCK), jnp.bfloat16) for size in sizes),
            *(pltpu.VMEM((steps, size, BLOCK), jnp.bfloat16) for size in sizes),
            *(dma((RING,)) for _ in sizes),
            *(dma((steps,)) for _ in sizes),
        ],
        compiler_params=pltpu.CompilerParams(
            collective_id=0, has_side_effects=True, vmem_limit_bytes=54 * 2**20
        ),
        cost_estimate=pl.CostEstimate(
            flops=2 * 2 * PASSES * part * 2 * width * model,
            bytes_accessed=PASSES * 2 * 2 * width * model,
            transcendentals=0,
        ),
    )(half, weight, bias)


def of_side(values, n_lat, side):
    stages = n_lat.bit_length() - 1
    tail = values.shape[1:]
    rows = values.shape[0] // n_lat // PASSES
    cut = values.reshape((n_lat // 2, 2, PASSES * rows) + tail)
    cut = lax.dynamic_index_in_dim(cut, side, 1, keepdims=False)
    cut = cut.reshape((2,) * (stages - 1) + (PASSES, rows) + tail)
    order = (stages - 1,) + tuple(range(stages - 2, -1, -1)) + tuple(range(stages, cut.ndim))
    return cut.transpose(order).reshape((PASSES * rows * n_lat // 2,) + tail)


def shards(
    resid_halves,
    enc_weight,
    enc_bias,
    jump_threshold,
    dec_weight,
    dec_bias,
    clamp_rows,
    clamp_feats,
    clamp_slots,
    clamp_values,
):
    n_lat = lax.axis_size("lat")
    group = lax.axis_index("layer")
    source = group // 2
    core = lax.rem(group, 2)
    tokens = resid_halves.shape[1]
    width = enc_weight.shape[2]
    lat_first = lax.axis_index("lat") * width

    def pick(stacked, at):
        return lax.dynamic_index_in_dim(stacked, at, 0, keepdims=False)

    my_bias = pick(enc_bias, source)
    my_thresh = pick(jump_threshold, source)
    my_slots = pick(clamp_slots, source)
    slot_hot = my_slots[:, None] == jnp.arange(clamp_values.shape[0], dtype=jnp.int32)[None, :]
    chosen = jnp.sum(jnp.where(slot_hot, clamp_values[None, :], 0.0), axis=1)
    row_hot = pick(clamp_rows, source)[:, None] == jnp.arange(tokens, dtype=jnp.int32)[None, :]
    feat_row = jnp.sum(jnp.where(row_hot, pick(clamp_feats, source)[:, None], 0), axis=0)
    value_row = jnp.sum(jnp.where(row_hot, chosen[:, None], 0.0), axis=0)
    feat_row = of_side(feat_row, n_lat, core)
    value_row = of_side(value_row, n_lat, core)

    partial_pre = jnp.dot(resid_halves[0], enc_weight[0], preferred_element_type=jnp.float32)
    partner = swapped(of_side(partial_pre, n_lat, 1 - core), "layer", 0)
    pre_act = of_side(partial_pre, n_lat, core) + partner + my_bias[None, :]
    ramp = jnp.clip((pre_act - my_thresh[None, :]) / 0.25 + 1.0, 0.0, 1.0)
    hit = (feat_row - lat_first)[:, None] == jnp.arange(width, dtype=jnp.int32)[None, :]
    half = jnp.where(hit, value_row[:, None], pre_act * ramp).astype(jnp.bfloat16)
    half = half.reshape(PASSES, 2, tokens // 4 // PASSES, width)
    return decode(half, dec_weight[0], dec_bias, n_lat)[None]


def solution(mesh):
    return jax.shard_map(
        shards,
        mesh=mesh,
        in_specs=(
            P("layer", None, None),
            P("layer", None, "lat"),
            P(None, "lat"),
            P(None, "lat"),
            P("layer", None, "lat", None),
            P("layer", None),
            P(),
            P(),
            P(),
            P(),
        ),
        out_specs=P("layer", "lat", None),
        check_vma=False,
    )
```
